32 devices in a mesh: grp: 4 (over z), blk: 8 (over y, x, core).
Axes of the slice: x: 2, y: 2, z: 4, core: 2. Of those that a mesh axis runs over, the one named last changes fastest.
Arguments:
- ancestor_inv: float32 [4, 6144, 3072], P('grp', 'blk'), as said below
- lower_block: float32 [4, 3840, 768], P('grp', 'blk'), may hold values from -0.009765625 to 0.009765625
- diag_inverse: float32 [4, 768, 768], P('grp', 'blk'), as said below
- row_index: int32 [4, 3840], P('grp'), may hold values from 0 to 6143, as said below
Outputs:
- sigma_rows: float32 [4, 3840, 768], P('grp', 'blk')
- sigma_diag: float32 [4, 768, 768], P('grp', 'blk')
The draws below stay inside these ranges and needn't reach their ends.
Inputs may be any that keep to these rules, and one draw needn't show every extreme that they name: `row_index`: for each child front: sorted increasing and distinct; exactly 480 entries fall in each aligned block of 768 consecutive indices, among them the block's first and last index. `diag_inverse`: lower triangular with a positive diagonal. `ancestor_inv`: each parent matrix assembled from its two column halves is symmetric.
All inputs are finite; a program needn't handle non-finite values.
Results may differ from the reference program's by a relative error of at most 0.0003.
Values sent between devices are 32-bit elements; how exact they have to be, the bound alone decides.
No kernel may reach another device: no remote copies, remote signals or barrier semaphores. Data moves between devices by JAX's collectives and lax.ppermute only.
A program may use at most 128 MiB of HBM per device.

```python
import math
import jax
import jax.numpy as jnp
from jax import lax

PA = 6144
R = 3840
B = 768
CHILDREN = 4
BLOCK = 768
PICK = 480


def draw_ancestor_inv(key, part):
    parent_keys = jax.random.split(key, CHILDREN // 2)

    def one_parent(parent_key):
        key_noise, key_diag = jax.random.split(parent_key, 2)
        entries = jax.random.normal(key_noise, (PA, PA), jnp.float32)
        symmetric = (entries + entries.T) * 1.41
        row_ids = lax.broadcasted_iota(jnp.int32, (PA, PA), 0)
        col_ids = lax.broadcasted_iota(jnp.int32, (PA, PA), 1)
        diagonal = jnp.exp(jax.random.uniform(key_diag, (PA,), jnp.float32, math.log(200.0), math.log(600.0)))
        matrix = jnp.where(row_ids == col_ids, diagonal[:, None], symmetric)
        return jnp.transpose(matrix.reshape(PA, 2, PA // 2), (1, 0, 2))
    halves = lax.map(one_parent, parent_keys)
    return halves.reshape(CHILDREN, PA, PA // 2)


def draw_diag_inverse(key, part):
    key_noise, key_diag = jax.random.split(key, 2)
    shape_all = (CHILDREN, B, B)
    noise = jax.random.normal(key_noise, shape_all, jnp.float32) * 0.05
    diagonal = jnp.exp(jax.random.uniform(key_diag, shape_all, jnp.float32, math.log(0.5), math.log(2.0)))
    row_ids = lax.broadcasted_iota(jnp.int32, shape_all, 1)
    col_ids = lax.broadcasted_iota(jnp.int32, shape_all, 2)
    lower_part = jnp.where(row_ids > col_ids, noise, jnp.zeros(shape_all, jnp.float32))
    return jnp.where(row_ids == col_ids, diagonal, lower_part)


def draw_row_index(key, part):
    count_blocks = R // PICK

    def one_block(block_key, block_id):
        shuffled = jax.random.permutation(block_key, BLOCK - 2).astype(jnp.int32) + 1
        middle = jnp.sort(shuffled[:PICK - 2])
        first = jnp.zeros((1,), jnp.int32)
        last = jnp.full((1,), BLOCK - 1, jnp.int32)
        chosen = jnp.concatenate([first, middle.astype(jnp.int32), last])
        return chosen.astype(jnp.int32) + block_id * BLOCK

    def one_child(child_key):
        block_keys = jax.random.split(child_key, count_blocks)
        blocks_out = jax.vmap(one_block)(block_keys, jnp.arange(count_blocks, dtype=jnp.int32))
        return blocks_out.reshape(R).astype(jnp.int32)
    return jax.vmap(one_child)(jax.random.split(key, CHILDREN)).astype(jnp.int32)


def block_scale(key, extent, cuts, smallest, top_value):
    factor_of = 1.0
    for axis_at, blocks in cuts:
        heights = jax.random.uniform(jax.random.fold_in(jax.random.fold_in(key, 6), axis_at), (blocks,), jnp.float32, smallest / len(cuts), top_value / len(cuts))
        factor_of = factor_of * jnp.repeat(jnp.exp(heights), extent[axis_at] // blocks).reshape((-1,) + (1,) * (len(extent) - 1 - axis_at))
    return factor_of


def centred(stream_key, shape, spread, limit, shards=(), kind=jnp.bfloat16):
    result = jax.random.normal(stream_key, shape, jnp.float32) * spread
    if len(shards) > 0:
        result = block_scale(stream_key, shape, shards, -0.22, 0.18) * result
    return jnp.clip(result, min=-limit, max=limit).astype(kind)


def setup_inputs(seed: int = 0) -> dict:
    keys = jax.random.split(jax.random.key(seed), 5)
    ancestor_inv = draw_ancestor_inv(jax.random.fold_in(keys[4], 71), 0)
    lower_block = centred(keys[1], (CHILDREN, R, B), 0.00065, 0.009765625, ((0, 4), (1, 8)), jnp.float32)
    diag_inverse = draw_diag_inverse(jax.random.fold_in(keys[4], 71), 0)
    row_index = draw_row_index(jax.random.fold_in(keys[4], 71), 0)
    return dict(ancestor_inv=ancestor_inv, lower_block=lower_block, diag_inverse=diag_inverse, row_index=row_index)


def reference(ancestor_inv, lower_block, diag_inverse, row_index):
    highest = lax.Precision.HIGHEST
    count = lower_block.shape[0]

    def one_child(item):
        child, lower, pivot, names = item
        pair = lax.dynamic_slice_in_dim(ancestor_inv, (child // 2) * 2, 2, 0)
        full = jnp.concatenate([pair[0], pair[1]], axis=1)
        ancestor = jnp.take(jnp.take(full, names, axis=0), names, axis=1)
        factor = jnp.dot(lower, pivot, precision=highest, preferred_element_type=jnp.float32)
        rows_out = -jnp.dot(ancestor, factor, precision=highest, preferred_element_type=jnp.float32)
        gram = jnp.dot(pivot.T, pivot, precision=highest, preferred_element_type=jnp.float32)
        diag_out = gram - jnp.dot(factor.T, rows_out, precision=highest, preferred_element_type=jnp.float32)
        return rows_out, diag_out

    child_ids = jnp.arange(count, dtype=jnp.int32)
    sigma_rows, sigma_diag = lax.map(one_child, (child_ids, lower_block, diag_inverse, row_index))
    return sigma_rows, sigma_diag
```

```python
import functools

import jax
import jax.numpy as jnp
from jax import lax
from jax.experimental import pallas as pl
from jax.experimental.pallas import tpu as pltpu
from jax.sharding import PartitionSpec as P

F32, BF16 = jnp.float32, jnp.bfloat16
TOP = 3.3895313892515355e38
DOWN, UP = 1.0 / 64.0, 64.0
NN = (((1,), (0,)), ((), ()))
TN = (((0,), (0,)), ((), ()))
VMEM = pl.BlockSpec(memory_space=pltpu.VMEM)
SMEM = pl.BlockSpec(memory_space=pltpu.SMEM)


def split(x):
    high = jnp.clip(x, -TOP, TOP).astype(BF16)
    return high, (x - high.astype(F32)).astype(BF16)


def dot1(a, b, dims=NN):
    return lax.dot_general(a, b, dims, preferred_element_type=F32)


def dot3(a, b, dims=NN):
    return dot1(a[0], b[0], dims) + dot1(a[0], b[1], dims) + dot1(a[1], b[0], dims)


def params(**more):
    return pltpu.CompilerParams(vmem_limit_bytes=48 * 2**20, **more)


def pick_kernel(info, rows_ref, cols_ref, tile_ref, high_ref, low_ref):
    @pl.when(info[0] == 1)
    def _():
        height, width = tile_ref.shape
        picked = rows_ref.shape[0]
        at_row = lax.broadcasted_iota(jnp.int32, (picked, height), 1)
        row_hot = (at_row == rows_ref[...]).astype(F32).astype(BF16)
        high, low = split(tile_ref[...])
        high = dot1(row_hot, high).astype(BF16)
        low = dot1(row_hot, low).astype(BF16)
        at_col = lax.broadcasted_iota(jnp.int32, (width, picked), 0)
        for q in range(cols_ref.shape[0]):
            col_hot = (at_col == cols_ref[q]).astype(F32).astype(BF16)
            high_ref[q] = dot1(high, col_hot).astype(BF16)
            low_ref[q] = dot1(low, col_hot).astype(BF16)


def pick(active, tile, rows, cols, group):
    height, all_cols = tile.shape
    blocks, picked = cols.shape
    width = all_cols // blocks * group
    out = jax.ShapeDtypeStruct((blocks, picked, picked), BF16)
    return pl.pallas_call(
        pick_kernel,
        grid_spec=pltpu.PrefetchScalarGridSpec(
            num_scalar_prefetch=1,
            grid=(blocks // group,),
            in_specs=[
                pl.BlockSpec((picked, 1), lambda i, info: (0, 0)),
                pl.BlockSpec((group, 1, picked), lambda i, info: (i, 0, 0)),
                pl.BlockSpec((height, width), lambda i, info: (0, i * info[0])),
            ],
            out_specs=[pl.BlockSpec((group, picked, picked), lambda i, info: (i * info[0], 0, 0))] * 2,
        ),
        out_shape=[out, out],
        compiler_params=params(),
        name="pick",
    )(active[None], rows[:, None], cols[:, None, :], tile)


def apply_kernel(info, high_ref, low_ref, *refs):
    pieces, out_ref = refs[:-1], refs[-1]
    step = pl.program_id(0)

    @pl.when(info[0] == 1)
    def _():
        for p, piece in enumerate(pieces):

            @pl.when(step == p)
            def _(p=p, piece=piece):
                part = dot3((high_ref[0], low_ref[0]), split(piece[...] * DOWN))
                out_ref[...] = part if p == 0 else out_ref[...] + part


def apply(active, me, high, low, pieces):
    blocks, picked, _ = high.shape
    width = pieces[0].shape[1]
    block = pl.BlockSpec(
        (1, picked, picked), lambda p, info: (lax.bitwise_xor(info[1], p * info[0]), 0, 0)
    )
    whole = pl.BlockSpec((picked, width), lambda p, info: (0, 0))
    return pl.pallas_call(
        apply_kernel,
        grid_spec=pltpu.PrefetchScalarGridSpec(
            num_scalar_prefetch=1,
            grid=(blocks,),
            in_specs=[block, block] + [whole] * blocks,
            out_specs=whole,
        ),
        out_shape=jax.ShapeDtypeStruct((picked, width), F32),
        compiler_params=params(),
        cost_estimate=pl.CostEstimate(
            flops=6 * blocks * picked * picked * width,
            bytes_accessed=blocks * (4 * picked * picked + 4 * picked * width),
            transcendentals=0,
        ),
        name="apply",
    )(jnp.stack([active, me]), high, low, *pieces)


def back_kernel(info, high_ref, low_ref, lower_ref, *out_refs):
    step = pl.program_id(0)
    chunks = len(out_refs) // 2

    @pl.when(info[0] == 1)
    def _():
        width = lower_ref.shape[1] // chunks
        pair = (high_ref[0], low_ref[0])
        for c in range(chunks):
            rhs = split(lower_ref[:, c * width : (c + 1) * width] * DOWN)
            part = dot3(pair, rhs, TN)
            for parity in range(2):

                @pl.when(step % 2 == parity)
                def _(part=part, ref=out_refs[2 * c + parity]):
                    ref[0] = part


def back(active, me, high, low, lower, chunks):
    blocks, picked, _ = high.shape
    total = lower.shape[1]
    width = total // chunks
    block = pl.BlockSpec(
        (1, picked, picked), lambda p, info: (lax.bitwise_xor(info[1], p * info[0]), 0, 0)
    )
    out = jax.ShapeDtypeStruct((blocks // 2, picked, width), F32)
    flat = pl.pallas_call(
        back_kernel,
        grid_spec=pltpu.PrefetchScalarGridSpec(
            num_scalar_prefetch=1,
            grid=(blocks,),
            in_specs=[block, block, pl.BlockSpec((picked, total), lambda p, info: (0, 0))],
            out_specs=[pl.BlockSpec((1, picked, width), lambda p, info: (p // 2 * info[0], 0, 0))]
            * (2 * chunks),
        ),
        out_shape=[out] * (2 * chunks),
        compiler_params=params(),
        cost_estimate=pl.CostEstimate(
            flops=6 * blocks * picked * picked * total,
            bytes_accessed=blocks * (4 * picked * picked + 4 * picked * total),
            transcendentals=0,
        ),
        name="back",
    )(jnp.stack([active, me]), high, low, lower)
    return [(flat[2 * c], flat[2 * c + 1]) for c in range(chunks)]


def factor_kernel(lower_ref, pivot_ref, high_ref, low_ref):
    high_ref[...], low_ref[...] = split(dot3(split(lower_ref[...]), split(pivot_ref[...])))


def factor_of(lower, pivot):
    out = jax.ShapeDtypeStruct(lower.shape, BF16)
    return pl.pallas_call(
        factor_kernel,
        in_specs=[VMEM, VMEM],
        out_specs=[VMEM, VMEM],
        out_shape=[out, out],
        compiler_params=params(),
        cost_estimate=pl.CostEstimate(
            flops=6 * lower.size * lower.shape[1], bytes_accessed=8 * lower.size, transcendentals=0
        ),
        name="factor",
    )(lower, pivot)


def finish_kernel(chunk, first, info, *refs):
    here_ref, there_ref, arrived_ref, pivot_ref, high_ref, low_ref = refs[:6]
    earlier = refs[6 : 6 + chunk[1] - 1 - chunk[0]]
    rows_ref, sum_ref, keep_ref, send_ref, cross_ref = refs[-5:]
    width = here_ref.shape[1]
    at = chunk[0] * width
    mine = jnp.where(info[0] == 1, here_ref[...], there_ref[...]) + arrived_ref[...]
    sum_ref[...] = mine
    result = dot3(split(mine), split(pivot_ref[at : at + width, at : at + width]))
    for k, ref in enumerate(earlier):
        low_at = (chunk[0] + 1 + k) * width
        result += dot3(split(ref[...]), split(pivot_ref[low_at : low_at + width, at : at + width]))
    result = result * UP
    rows_ref[...] = -result
    cross_ref[...] = dot3((high_ref[...], low_ref[...]), split(result), TN)
    height = keep_ref.shape[1]
    for q in range(keep_ref.shape[0]):
        for parity, ref in enumerate((keep_ref, send_ref)):
            place = lax.bitwise_xor(info[1], 2 * q + parity)
            ref[q] = cross_ref[pl.ds(pl.multiple_of(place * height, 8), height), :]


def finish(chunk, count, same, blk, parts, here, there, arrived, pivot, factor, earlier, so_far):
    picked, width = here.shape
    order = pivot.shape[0]
    height = order // parts
    piece = jax.ShapeDtypeStruct((parts // 2, height, width), F32)
    operands = [jnp.stack([same, blk]), here, there, arrived, pivot, *factor, *earlier]
    in_specs = [SMEM] + [VMEM] * (len(operands) - 1)
    aliases = {}
    if so_far is not None:
        aliases = {len(operands): 0}
        operands.append(so_far)
        in_specs.append(pl.BlockSpec(memory_space=pl.ANY))
    return pl.pallas_call(
        functools.partial(finish_kernel, (chunk, count), so_far is None),
        grid=(1,),
        in_specs=in_specs,
        out_specs=[pl.BlockSpec((picked, width), lambda i: (0, chunk)), VMEM, VMEM, VMEM],
        out_shape=[
            jax.ShapeDtypeStruct((picked, order), F32),
            jax.ShapeDtypeStruct((picked, width), F32),
            piece,
            piece,
        ],
        scratch_shapes=[pltpu.VMEM((order, width), F32)],
        input_output_aliases=aliases,
        compiler_params=params(),
        cost_estimate=pl.CostEstimate(
            flops=6 * picked * width * (order + (1 + len(earlier)) * width),
            bytes_accessed=4 * (order * order + 4 * picked * width),
            transcendentals=0,
        ),
        name="finish",
    )(*operands)


def shards(ancestor_inv, lower_block, diag_inverse, row_index):
    grps, blks = lax.axis_size("grp"), lax.axis_size("blk")
    half = blks // 2
    tile, lower, names = ancestor_inv[0], lower_block[0], row_index[0]
    tile_rows, half_cols = tile.shape
    picked, order = lower.shape
    blk, grp = lax.axis_index("blk"), lax.axis_index("grp")
    side = grp % 2
    me = blk % half
    is_same = blk // half == side
    same = is_same.astype(jnp.int32)
    other = 1 - same
    one = jnp.ones((), jnp.int32)
    chunks = 3
    width = order // chunks

    everyone = [(g, b) for g in range(grps) for b in range(blks)]
    sames = [(g, b) for g, b in everyone if b // half == g % 2]
    others = [(g, b) for g, b in everyone if b // half != g % 2]

    def move(x, pairs):
        perm = [(g * blks + b, h * blks + c) for (g, b), (h, c) in pairs]
        return lax.ppermute(x, ("grp", "blk"), perm)

    def across(x, who, stride):
        return move(x, [((g, b), (g, b ^ stride)) for g, b in who])

    onward = [((g, b), (g, b ^ half)) for g, b in sames] + [((g, b), (g ^ 1, b)) for g, b in others]
    backward = [(to, at) for at, to in onward]

    def gather(x, who):
        pieces = {0: x}
        strides = [1 << s for s in range(1, half.bit_length() - 1)] + [1]
        for stride in strides:
            pieces.update({p ^ stride: across(piece, who, stride) for p, piece in list(pieces.items())})
        return [pieces[p] for p in range(half)]

    sibling_names = lax.ppermute(names, "grp", [(g, g ^ 1) for g in range(grps)])
    pivot = lax.all_gather(diag_inverse[0], "blk", axis=0, tiled=True)
    own_chunks = [lower[:, c * width : (c + 1) * width] for c in range(chunks)]
    order_of = list(range(chunks))[::-1]
    sent_on = {c: move(own_chunks[c], onward) for c in order_of}
    far = {c: gather(sent_on[c], everyone) for c in order_of}
    near = {c: gather(own_chunks[c], sames) for c in order_of}

    group = max(1, 768 // tile_rows)
    while half % group:
        group //= 2

    def lists(which):
        rows = lax.dynamic_slice_in_dim(which, blk * picked, picked) - blk * tile_rows
        cols = lax.dynamic_slice_in_dim(which, side * half * picked, half * picked)
        cols = cols.reshape(half, picked) - (side * half + jnp.arange(half)[:, None]) * tile_rows
        return rows, cols + (jnp.arange(half)[:, None] % group) * tile_rows

    own_pick = pick(same, tile, *lists(names), group)
    far_pick = pick(one, tile, *lists(jnp.where(is_same, sibling_names, names)), group)

    partial = back(other, me, *far_pick, lower, chunks)
    factor = factor_of(lower, pivot)

    earlier, so_far, crosses = [], None, {}
    for c in order_of:
        there = apply(one, me, *far_pick, far[c])
        keep, send = partial[c]
        left = keep + across(send, others, 1)
        for s in range(1, half.bit_length() - 1):
            stride = 1 << s
            left = left.reshape(left.shape[0] // 2, 2, picked, width)
            left = left[:, 0] + across(left[:, 1], others, stride)
        arrived = move(jnp.where(is_same, there, left[0]), backward)
        here = apply(same, me, *own_pick, near[c])
        so_far, total, keep, send = finish(
            c, chunks, same, blk, blks, here, there, arrived, pivot, factor, earlier, so_far
        )
        earlier = [total] + earlier
        left = keep + across(send, everyone, 1)
        crosses[c] = left[0] + sum(across(left[q], everyone, 2 * q) for q in range(1, half))

    cross = jnp.concatenate([crosses[c] for c in range(chunks)], axis=1)
    height = order // blks
    gram_cols = lax.dynamic_slice_in_dim(pivot, blk * height, height, 1)
    gram = jnp.einsum("ar,ac->rc", gram_cols, pivot, precision=lax.Precision.HIGHEST)
    return so_far[None], (gram + cross)[None]


def solution(mesh):
    in_specs = (P("grp", "blk", None), P("grp", "blk", None), P("grp", "blk", None), P("grp", None))
    out_specs = (P("grp", "blk", None), P("grp", "blk", None))
    return jax.shard_map(shards, mesh=mesh, in_specs=in_specs, out_specs=out_specs, check_vma=False)
```

```python
import functools

import jax
import jax.numpy as jnp
from jax import lax
from jax.experimental import pallas as pl
from jax.experimental.pallas import tpu as pltpu
from jax.sharding import PartitionSpec as P

F32, BF16 = jnp.float32, jnp.bfloat16
TOP = 3.3895313892515355e38
COST = 3.3e6
DOWN, UP = 1.0 / 64.0, 64.0
NN = (((1,), (0,)), ((), ()))
VMEM = pl.BlockSpec(memory_space=pltpu.VMEM)
ANY = pl.BlockSpec(memory_space=pl.ANY)
HBM = pl.BlockSpec(memory_space=pltpu.HBM)
SMEM = pl.BlockSpec(memory_space=pltpu.SMEM)


def split(x):
    high = jnp.clip(x, -TOP, TOP).astype(BF16)
    return high, (x - high.astype(F32)).astype(BF16)


def dot1(a, b, dims=NN):
    return lax.dot_general(a, b, dims, preferred_element_type=F32)


def dot3(a, b, dims=NN):
    return dot1(a[0], b[0], dims) + dot1(a[0], b[1], dims) + dot1(a[1], b[0], dims)


def wide3(high, low, rhs):
    width = rhs[0].shape[1]
    pair = dot1(high, jnp.concatenate(rhs, axis=1))
    return pair[:, :width] + pair[:, width:] + dot1(low, rhs[0])


def cost(microseconds):
    return pl.CostEstimate(
        flops=0, bytes_accessed=int(microseconds * COST), transcendentals=0
    )


def params(mib):
    return pltpu.CompilerParams(vmem_limit_bytes=mib * 2**20)


def load_tile(tile_ref, slots, sems, step, steps):
    width = slots.shape[2]

    def copy(at):
        slot = at % 2
        source = tile_ref.at[:, pl.ds(pl.multiple_of(at * width, 128), width)]
        return pltpu.make_async_copy(source, slots.at[slot], sems.at[slot])

    @pl.when(step == 0)
    def _():
        copy(step).start()

    @pl.when(step + 1 < steps)
    def _():
        copy(step + 1).start()

    copy(step).wait()
    return slots[step % 2]


def hot_rows(rows_ref, hot_ref):
    at_row = lax.broadcasted_iota(jnp.int32, hot_ref.shape, 1)
    hot_ref[...] = (at_row == rows_ref[...]).astype(F32).astype(BF16)


def pick_block(block, cols_ref, hot_ref, high_ref, low_ref):
    picked = hot_ref.shape[0]
    pair = split(block)
    both = jnp.concatenate([dot1(hot_ref[...], piece) for piece in pair], axis=0).astype(BF16)
    at_col = lax.broadcasted_iota(jnp.int32, (block.shape[1], picked), 0)
    for q in range(cols_ref.shape[0]):
        col_hot = (at_col == cols_ref[q]).astype(F32).astype(BF16)
        result = dot1(both, col_hot)
        high_ref[q] = result[:picked].astype(BF16)
        low_ref[q] = result[picked:].astype(BF16)


def pick_kernel(rows_ref, cols_ref, tile_ref, high_ref, low_ref, hot_ref, slots, sems):
    step = pl.program_id(0)

    @pl.when(step == 0)
    def _():
        hot_rows(rows_ref, hot_ref)

    block = load_tile(tile_ref, slots, sems, step, pl.num_programs(0))
    pick_block(block, cols_ref, hot_ref, high_ref, low_ref)


def pick(tile, rows, cols, group):
    height, all_cols = tile.shape
    blocks, picked = cols.shape
    width = all_cols // blocks * group
    out = jax.ShapeDtypeStruct((blocks, picked, picked), BF16)
    return pl.pallas_call(
        pick_kernel,
        grid=(blocks // group,),
        in_specs=[
            pl.BlockSpec((picked, 1), lambda i: (0, 0)),
            pl.BlockSpec((group, 1, picked), lambda i: (i, 0, 0)),
            HBM,
        ],
        out_specs=[pl.BlockSpec((group, picked, picked), lambda i: (i, 0, 0))] * 2,
        scratch_shapes=[
            pltpu.VMEM((picked, height), BF16),
            pltpu.VMEM((2, height, width), F32),
            pltpu.SemaphoreType.DMA((2,)),
        ],
        out_shape=[out] * 2,
        compiler_params=params(56),
        cost_estimate=cost(10),
        name="pick",
    )(rows[:, None], cols[:, None, :], tile)


def second_kernel(steps, info, rows_ref, cols_ref, tile_ref, q_high, q_low, lower_ref, *refs):
    high_ref, low_ref = refs[:2]
    hot_ref, slots, sems, lower_high, lower_low = refs[-5:]
    out_refs = refs[2:-5]
    chunks = len(out_refs) // 2
    width = lower_ref.shape[1] // chunks
    step = pl.program_id(0)

    @pl.when((info[0] == 1) & (step == 0))
    def _():
        hot_rows(rows_ref, hot_ref)

    @pl.when((info[0] == 1) & (step < steps))
    def _():
        block = load_tile(tile_ref, slots, sems, step, steps)
        pick_block(block, cols_ref, hot_ref, high_ref, low_ref)

    @pl.when((info[0] == 0) & (step == 0))
    def _():
        lower_high[...], lower_low[...] = split(lower_ref[...] * DOWN)

    @pl.when(info[0] == 0)
    def _():
        high, low = jnp.transpose(q_high[0]), jnp.transpose(q_low[0])
        full = dot1(high, lower_high[...]) + dot1(high, lower_low[...]) + dot1(low, lower_high[...])
        for parity in range(2):

            @pl.when(step % 2 == parity)
            def _(parity=parity):
                for c in range(chunks):
                    out_refs[2 * c + parity][0] = full[:, c * width : (c + 1) * width]


def second(same, me, tile, rows, cols, group, high, low, lower, chunks):
    height, all_cols = tile.shape
    blocks, picked = cols.shape
    total = lower.shape[1]
    width = all_cols // blocks * group
    steps = blocks // group
    out = jax.ShapeDtypeStruct((blocks, picked, picked), BF16)
    back = jax.ShapeDtypeStruct((blocks // 2, picked, total // chunks), F32)

    def at_pick(p, info):
        return (jnp.minimum(p, steps - 1) * info[0], 0, 0)

    def at_block(p, info):
        return (lax.bitwise_xor(info[1], p * (1 - info[0])), 0, 0)

    def at_back(p, info):
        return (p // 2 * (1 - info[0]), 0, 0)

    flat = pl.pallas_call(
        functools.partial(second_kernel, steps),
        grid_spec=pltpu.PrefetchScalarGridSpec(
            num_scalar_prefetch=1,
            grid=(blocks,),
            in_specs=[
                pl.BlockSpec((picked, 1), lambda p, info: (0, 0)),
                pl.BlockSpec((group, 1, picked), at_pick),
                HBM,
                pl.BlockSpec((1, picked, picked), at_block),
                pl.BlockSpec((1, picked, picked), at_block),
                pl.BlockSpec((picked, total), lambda p, info: (0, 0)),
            ],
            out_specs=[pl.BlockSpec((group, picked, picked), at_pick)] * 2
            + [pl.BlockSpec((1, picked, total // chunks), at_back)] * (2 * chunks),
            scratch_shapes=[
                pltpu.VMEM((picked, height), BF16),
                pltpu.VMEM((2, height, width), F32),
                pltpu.SemaphoreType.DMA((2,)),
            ]
            + [pltpu.VMEM((picked, total), BF16)] * 2,
        ),
        out_shape=[out] * 2 + [back] * (2 * chunks),
        compiler_params=params(56),
        cost_estimate=cost(10),
        name="second",
    )(jnp.stack([same, me]), rows[:, None], cols[:, None, :], tile, high, low, lower)
    return flat[:2], [(flat[2 + 2 * c], flat[3 + 2 * c]) for c in range(chunks)]


def apply_kernel(info, high_ref, low_ref, *refs):
    pieces, out_ref = refs[:-1], refs[-1]
    step = pl.program_id(0)

    @pl.when(info[0] == 1)
    def _():
        for p, piece in enumerate(pieces):

            @pl.when(step == p)
            def _(p=p, piece=piece):
                part = wide3(high_ref[0], low_ref[0], split(piece[...] * DOWN))
                out_ref[...] = part if p == 0 else out_ref[...] + part


def apply(active, me, high, low, pieces):
    blocks, picked, _ = high.shape
    width = pieces[0].shape[1]
    block = pl.BlockSpec(
        (1, picked, picked), lambda p, info: (lax.bitwise_xor(info[1], p * info[0]), 0, 0)
    )
    whole = pl.BlockSpec((picked, width), lambda p, info: (0, 0))
    return pl.pallas_call(
        apply_kernel,
        grid_spec=pltpu.PrefetchScalarGridSpec(
            num_scalar_prefetch=1,
            grid=(blocks,),
            in_specs=[block, block] + [whole] * blocks,
            out_specs=whole,
        ),
        out_shape=jax.ShapeDtypeStruct((picked, width), F32),
        compiler_params=params(12),
        cost_estimate=cost(4.5),
        name="apply",
    )(jnp.stack([active, me]), high, low, *pieces)


def factor_kernel(lower_ref, pivot_ref, high_ref, low_ref):
    full = dot3(split(lower_ref[...]), split(pivot_ref[...]))
    high_ref[...], low_ref[...] = split(jnp.transpose(full))


def factor_of(lower, pivot):
    out = jax.ShapeDtypeStruct(lower.shape[::-1], BF16)
    return pl.pallas_call(
        factor_kernel,
        in_specs=[VMEM, VMEM],
        out_specs=[VMEM, VMEM],
        out_shape=[out, out],
        compiler_params=params(16),
        cost_estimate=cost(2.2),
        name="factor",
    )(lower, pivot)


def finish_kernel(chunk, count, info, *refs):
    local_ref, arrived_ref, pivot_ref, high_ref, low_ref = refs[:5]
    earlier = refs[5 : 5 + count - 1 - chunk]
    rows_ref, sum_ref, keep_ref, send_ref, cross_ref = refs[-5:]
    width = local_ref.shape[1]
    at = chunk * width
    mine = local_ref[...] + arrived_ref[...]
    sum_ref[...] = mine
    result = dot3(split(mine), split(pivot_ref[at : at + width, at : at + width]))
    for k, ref in enumerate(earlier):
        low_at = (chunk + 1 + k) * width
        result += dot3(split(ref[...]), split(pivot_ref[low_at : low_at + width, at : at + width]))
    result = result * UP
    rows_ref[...] = -result
    cross_ref[...] = dot3((high_ref[...], low_ref[...]), split(result))
    height = keep_ref.shape[1]
    for q in range(keep_ref.shape[0]):
        for parity, ref in enumerate((keep_ref, send_ref)):
            place = lax.bitwise_xor(info[0], 2 * q + parity)
            ref[q] = cross_ref[pl.ds(pl.multiple_of(place * height, 8), height), :]


def finish(chunk, count, blk, parts, local, arrived, pivot, factor, earlier, so_far):
    picked, width = local.shape
    order = pivot.shape[0]
    height = order // parts
    piece = jax.ShapeDtypeStruct((parts // 2, height, width), F32)
    operands = [blk[None], local, arrived, pivot, *factor, *earlier]
    in_specs = [SMEM] + [VMEM] * (len(operands) - 1)
    aliases = {}
    if so_far is not None:
        aliases = {len(operands): 0}
        operands.append(so_far)
        in_specs.append(ANY)
    return pl.pallas_call(
        functools.partial(finish_kernel, chunk, count),
        grid=(1,),
        in_specs=in_specs,
        out_specs=[pl.BlockSpec((picked, width), lambda i: (0, chunk)), VMEM, VMEM, VMEM],
        out_shape=[
            jax.ShapeDtypeStruct((picked, order), F32),
            jax.ShapeDtypeStruct((picked, width), F32),
            piece,
            piece,
        ],
        scratch_shapes=[pltpu.VMEM((order, width), F32)],
        input_output_aliases=aliases,
        compiler_params=params(20),
        cost_estimate=cost(5),
        name="finish",
    )(*operands)


def shards(ancestor_inv, lower_block, diag_inverse, row_index):
    grps, blks = lax.axis_size("grp"), lax.axis_size("blk")
    half = blks // 2
    tile, lower, names = ancestor_inv[0], lower_block[0], row_index[0]
    tile_rows, half_cols = tile.shape
    picked, order = lower.shape
    blk, grp = lax.axis_index("blk"), lax.axis_index("grp")
    side = grp % 2
    me = blk % half
    is_same = blk // half == side
    same = is_same.astype(jnp.int32)
    one = jnp.ones((), jnp.int32)
    chunks = 2
    width = order // chunks

    everyone = [(g, b) for g in range(grps) for b in range(blks)]
    sames = [(g, b) for g, b in everyone if b // half == g % 2]
    others = [(g, b) for g, b in everyone if b // half != g % 2]

    def move(x, pairs):
        perm = [(g * blks + b, h * blks + c) for (g, b), (h, c) in pairs]
        return lax.ppermute(x, ("grp", "blk"), perm)

    def across(x, who, stride):
        return move(x, [((g, b), (g, b ^ stride)) for g, b in who])

    def after(*arrays):
        return lax.optimization_barrier(arrays)

    onward = [((g, b), (g, b ^ half)) for g, b in sames] + [((g, b), (g ^ 1, b)) for g, b in others]
    backward = [(to, at) for at, to in onward]

    def on_core(x, who=everyone):
        return across(x, who, 1)

    def spread(arrays, who):
        arrays.update({p ^ 1: on_core(x, who) for p, x in list(arrays.items())})
        return [arrays[p] for p in range(half)]

    chips = [2 * s for s in range(half // 2)]

    def chip_gather(x, who):
        return {0: x} | {p: across(x, who, p) for p in chips[1:]}

    own = lax.optimization_barrier([lower[:, c * width : (c + 1) * width] for c in range(chunks)])
    high, low = chunks - 1, 0
    sent = {c: move(own[c], onward) for c in (high, low)}
    near = {high: chip_gather(own[high], sames)}
    sibling_names = lax.ppermute(names, "grp", [(g, g ^ 1) for g in range(grps)])
    pivot = lax.all_gather(diag_inverse[0], "blk", axis=0, tiled=True)

    group = max(1, 768 // tile_rows)
    while half % group:
        group //= 2

    def lists(which):
        rows = lax.dynamic_slice_in_dim(which, blk * picked, picked) - blk * tile_rows
        cols = lax.dynamic_slice_in_dim(which, side * half * picked, half * picked)
        cols = cols.reshape(half, picked) - (side * half + jnp.arange(half)[:, None]) * tile_rows
        return rows, cols + (jnp.arange(half)[:, None] % group) * tile_rows

    own_pick = pick(tile, *lists(names), group)
    sibling_names, own_pick, sent[high] = after(sibling_names, own_pick, sent[high])
    sib_pick, partial = second(
        same, me, tile, *lists(sibling_names), group, *own_pick, lower, chunks
    )

    def sum_cores(keep, send):
        got = on_core(send, others)
        return {i: keep[i] + got[i] for i in range(half // 2)}

    def sum_chips(places):
        for s in range(half.bit_length() - 2):
            for i in [i for i in places if i >> s & 1]:
                places[i ^ 1 << s] += across(places.pop(i), others, 2 << s)
        return places[0]

    sib_high = chip_gather(sent[high], sames)
    partial[high], sib_high, near[high], sent[low] = after(
        partial[high], sib_high, near[high], sent[low]
    )
    partial[low], sent[low] = after(partial[low], sent[low])
    sums = {c: sum_cores(*partial[c]) for c in (high, low)}
    away = {c: {i: x for i, x in sums[c].items() if i} for c in sums}
    away, sib_high = after(away, sib_high)
    back_sum = {c: sum_chips(away[c] | {0: sums[c][0]}) for c in (high, low)}
    sib = {high: spread(sib_high, sames)}
    sib_low = chip_gather(sent[low], sames)

    passed = {p: across(x, sames, half) for p, x in near[high].items() if p}
    high_parts = {p: jnp.where(is_same, x, passed[p]) if p else jnp.where(is_same, x, sent[high]) for p, x in near[high].items()}
    low_parts = chip_gather(jnp.where(is_same, own[low], sent[low]), everyone)

    result = apply(same, me, *sib_pick, sib[high])
    arrived = {high: move(jnp.where(is_same, result, back_sum[high]), backward)}
    result, sib_low = after(result, sib_low)
    sib[low], back_sum[low] = after(spread(sib_low, sames), back_sum[low])
    result = apply(same, me, *sib_pick, sib[low])
    arrived[low] = move(jnp.where(is_same, result, back_sum[low]), backward)

    result, high_parts, pivot = after(result, high_parts, pivot)

    height = order // blks
    gram_cols = lax.dynamic_slice_in_dim(pivot, blk * height, height, 1)
    gram = jnp.einsum("ar,ac->rc", gram_cols, pivot, precision=lax.Precision.HIGHEST)
    factor = factor_of(lower, pivot)
    local = apply(one, me, *own_pick, spread(high_parts, everyone))
    factor, gram, local = after(factor, gram, local)
    so_far, total, keep, send = finish(
        high, chunks, blk, blks, local, arrived[high], pivot, factor, [], None
    )

    def scatter(keep, send):
        left = keep + on_core(send)
        return left[0] + sum(across(left[q], everyone, 2 * q) for q in range(1, half))

    crosses = {high: scatter(keep, send)}
    total, low_parts = after(total, low_parts)
    local = apply(one, me, *own_pick, spread(low_parts, everyone))
    so_far, _, keep, send = finish(
        low, chunks, blk, blks, local, arrived[low], pivot, factor, [total], so_far
    )
    crosses[low] = scatter(keep, send)

    cross = jnp.concatenate([crosses[c] for c in range(chunks)], axis=1)
    return so_far[None], (gram + cross)[None]


def solution(mesh):
    in_specs = (P("grp", "blk", None), P("grp", "blk", None), P("grp", "blk", None), P("grp", None))
    out_specs = (P("grp", "blk", None), P("grp", "blk", None))
    return jax.shard_map(shards, mesh=mesh, in_specs=in_specs, out_specs=out_specs, check_vma=False)
```

```python
import functools

import jax
import jax.numpy as jnp
from jax import lax
from jax.experimental import pallas as pl
from jax.experimental.pallas import tpu as pltpu
from jax.sharding import PartitionSpec as P

F32, BF16 = jnp.float32, jnp.bfloat16
TOP = 3.3895313892515355e38
COST = 3.3e6
DOWN, UP = 1.0 / 64.0, 64.0
NN = (((1,), (0,)), ((), ()))
VMEM = pl.BlockSpec(memory_space=pltpu.VMEM)
ANY = pl.BlockSpec(memory_space=pl.ANY)
HBM = pl.BlockSpec(memory_space=pltpu.HBM)
SMEM = pl.BlockSpec(memory_space=pltpu.SMEM)


def split(x):
    high = jnp.clip(x, -TOP, TOP).astype(BF16)
    return high, (x - high.astype(F32)).astype(BF16)


def dot1(a, b, dims=NN):
    return lax.dot_general(a, b, dims, preferred_element_type=F32)


def dot3(a, b, dims=NN):
    return dot1(a[0], b[0], dims) + dot1(a[0], b[1], dims) + dot1(a[1], b[0], dims)


def wide3(high, low, rhs):
    width = rhs[0].shape[1]
    pair = dot1(high, jnp.concatenate(rhs, axis=1))
    return pair[:, :width] + pair[:, width:] + dot1(low, rhs[0])


def cost(microseconds):
    return pl.CostEstimate(
        flops=0, bytes_accessed=int(microseconds * COST), transcendentals=0
    )


def params(mib):
    return pltpu.CompilerParams(vmem_limit_bytes=mib * 2**20)


def load_tile(tile_ref, slots, sems, step, steps):
    width = slots.shape[2]

    def copy(at):
        slot = at % 2
        source = tile_ref.at[:, pl.ds(pl.multiple_of(at * width, 128), width)]
        return pltpu.make_async_copy(source, slots.at[slot], sems.at[slot])

    @pl.when(step == 0)
    def _():
        copy(step).start()

    @pl.when(step + 1 < steps)
    def _():
        copy(step + 1).start()

    copy(step).wait()
    return slots[step % 2]


def hot_rows(rows_ref, hot_ref):
    at_row = lax.broadcasted_iota(jnp.int32, hot_ref.shape, 1)
    hot_ref[...] = (at_row == rows_ref[...]).astype(F32).astype(BF16)


def pick_block(block, cols_ref, hot_ref, high_ref, low_ref):
    picked = hot_ref.shape[0]
    pair = split(block)
    both = jnp.concatenate([dot1(hot_ref[...], piece) for piece in pair], axis=0).astype(BF16)
    at_col = lax.broadcasted_iota(jnp.int32, (block.shape[1], picked), 0)
    for q in range(cols_ref.shape[0]):
        col_hot = (at_col == cols_ref[q]).astype(F32).astype(BF16)
        result = dot1(both, col_hot)
        high_ref[q] = result[:picked].astype(BF16)
        low_ref[q] = result[picked:].astype(BF16)


def pick_kernel(rows_ref, cols_ref, tile_ref, high_ref, low_ref, hot_ref, slots, sems):
    step = pl.program_id(0)

    @pl.when(step == 0)
    def _():
        hot_rows(rows_ref, hot_ref)

    block = load_tile(tile_ref, slots, sems, step, pl.num_programs(0))
    pick_block(block, cols_ref, hot_ref, high_ref, low_ref)


def pick(tile, rows, cols, group):
    height, all_cols = tile.shape
    blocks, picked = cols.shape
    width = all_cols // blocks * group
    out = jax.ShapeDtypeStruct((blocks, picked, picked), BF16)
    return pl.pallas_call(
        pick_kernel,
        grid=(blocks // group,),
        in_specs=[
            pl.BlockSpec((picked, 1), lambda i: (0, 0)),
            pl.BlockSpec((group, 1, picked), lambda i: (i, 0, 0)),
            HBM,
        ],
        out_specs=[pl.BlockSpec((group, picked, picked), lambda i: (i, 0, 0))] * 2,
        scratch_shapes=[
            pltpu.VMEM((picked, height), BF16),
            pltpu.VMEM((2, height, width), F32),
            pltpu.SemaphoreType.DMA((2,)),
        ],
        out_shape=[out] * 2,
        compiler_params=params(56),
        cost_estimate=cost(10),
        name="pick",
    )(rows[:, None], cols[:, None, :], tile)


def second_kernel(steps, info, rows_ref, cols_ref, tile_ref, q_high, q_low, lower_ref, *refs):
    high_ref, low_ref = refs[:2]
    hot_ref, slots, sems, lower_high, lower_low = refs[-5:]
    out_refs = refs[2:-5]
    chunks = len(out_refs) // 2
    width = lower_ref.shape[1] // chunks
    step = pl.program_id(0)

    @pl.when((info[0] == 1) & (step == 0))
    def _():
        hot_rows(rows_ref, hot_ref)

    @pl.when((info[0] == 1) & (step < steps))
    def _():
        block = load_tile(tile_ref, slots, sems, step, steps)
        pick_block(block, cols_ref, hot_ref, high_ref, low_ref)

    @pl.when((info[0] == 0) & (step == 0))
    def _():
        lower_high[...], lower_low[...] = split(lower_ref[...] * DOWN)

    @pl.when(info[0] == 0)
    def _():
        high, low = jnp.transpose(q_high[0]), jnp.transpose(q_low[0])
        full = dot1(high, lower_high[...]) + dot1(high, lower_low[...]) + dot1(low, lower_high[...])
        for parity in range(2):

            @pl.when(step % 2 == parity)
            def _(parity=parity):
                for c in range(chunks):
                    out_refs[2 * c + parity][0] = full[:, c * width : (c + 1) * width]


def second(same, me, tile, rows, cols, group, high, low, lower, chunks):
    height, all_cols = tile.shape
    blocks, picked = cols.shape
    total = lower.shape[1]
    width = all_cols // blocks * group
    steps = blocks // group
    out = jax.ShapeDtypeStruct((blocks, picked, picked), BF16)
    back = jax.ShapeDtypeStruct((blocks // 2, picked, total // chunks), F32)

    def at_pick(p, info):
        return (jnp.minimum(p, steps - 1) * info[0], 0, 0)

    def at_block(p, info):
        return (lax.bitwise_xor(info[1], p * (1 - info[0])), 0, 0)

    def at_back(p, info):
        return (p // 2 * (1 - info[0]), 0, 0)

    flat = pl.pallas_call(
        functools.partial(second_kernel, steps),
        grid_spec=pltpu.PrefetchScalarGridSpec(
            num_scalar_prefetch=1,
            grid=(blocks,),
            in_specs=[
                pl.BlockSpec((picked, 1), lambda p, info: (0, 0)),
                pl.BlockSpec((group, 1, picked), at_pick),
                HBM,
                pl.BlockSpec((1, picked, picked), at_block),
                pl.BlockSpec((1, picked, picked), at_block),
                pl.BlockSpec((picked, total), lambda p, info: (0, 0)),
            ],
            out_specs=[pl.BlockSpec((group, picked, picked), at_pick)] * 2
            + [pl.BlockSpec((1, picked, total // chunks), at_back)] * (2 * chunks),
            scratch_shapes=[
                pltpu.VMEM((picked, height), BF16),
                pltpu.VMEM((2, height, width), F32),
                pltpu.SemaphoreType.DMA((2,)),
            ]
            + [pltpu.VMEM((picked, total), BF16)] * 2,
        ),
        out_shape=[out] * 2 + [back] * (2 * chunks),
        compiler_params=params(56),
        cost_estimate=cost(10),
        name="second",
    )(jnp.stack([same, me]), rows[:, None], cols[:, None, :], tile, high, low, lower)
    return flat[:2], [(flat[2 + 2 * c], flat[3 + 2 * c]) for c in range(chunks)]


def apply_kernel(info, high_ref, low_ref, *refs):
    pieces, out_ref = refs[:-1], refs[-1]
    step = pl.program_id(0)

    @pl.when(info[0] == 1)
    def _():
        for p, piece in enumerate(pieces):

            @pl.when(step == p)
            def _(p=p, piece=piece):
                part = wide3(high_ref[0], low_ref[0], split(piece[...] * DOWN))
                out_ref[...] = part if p == 0 else out_ref[...] + part


def apply(active, me, high, low, pieces):
    blocks, picked, _ = high.shape
    width = pieces[0].shape[1]
    block = pl.BlockSpec(
        (1, picked, picked), lambda p, info: (lax.bitwise_xor(info[1], p * info[0]), 0, 0)
    )
    whole = pl.BlockSpec((picked, width), lambda p, info: (0, 0))
    return pl.pallas_call(
        apply_kernel,
        grid_spec=pltpu.PrefetchScalarGridSpec(
            num_scalar_prefetch=1,
            grid=(blocks,),
            in_specs=[block, block] + [whole] * blocks,
            out_specs=whole,
        ),
        out_shape=jax.ShapeDtypeStruct((picked, width), F32),
        compiler_params=params(12),
        cost_estimate=cost(4.5),
        name="apply",
    )(jnp.stack([active, me]), high, low, *pieces)


def factor_kernel(lower_ref, pivot_ref, high_ref, low_ref):
    full = dot3(split(lower_ref[...]), split(pivot_ref[...]))
    high_ref[...], low_ref[...] = split(jnp.transpose(full))


def factor_of(lower, pivot):
    out = jax.ShapeDtypeStruct(lower.shape[::-1], BF16)
    return pl.pallas_call(
        factor_kernel,
        in_specs=[VMEM, VMEM],
        out_specs=[VMEM, VMEM],
        out_shape=[out, out],
        compiler_params=params(16),
        cost_estimate=cost(2.2),
        name="factor",
    )(lower, pivot)


def finish_kernel(chunk, count, info, *refs):
    local_ref, arrived_ref, pivot_ref, high_ref, low_ref = refs[:5]
    earlier = refs[5 : 5 + count - 1 - chunk]
    rows_ref, sum_ref, keep_ref, send_ref, cross_ref = refs[-5:]
    width = local_ref.shape[1]
    at = chunk * width
    mine = local_ref[...] + arrived_ref[...]
    sum_ref[...] = mine
    result = dot3(split(mine), split(pivot_ref[at : at + width, at : at + width]))
    for k, ref in enumerate(earlier):
        low_at = (chunk + 1 + k) * width
        result += dot3(split(ref[...]), split(pivot_ref[low_at : low_at + width, at : at + width]))
    result = result * UP
    rows_ref[...] = -result
    cross_ref[...] = dot3((high_ref[...], low_ref[...]), split(result))
    height = keep_ref.shape[1]
    for q in range(keep_ref.shape[0]):
        for parity, ref in enumerate((keep_ref, send_ref)):
            place = lax.bitwise_xor(info[0], 2 * q + parity)
            ref[q] = cross_ref[pl.ds(pl.multiple_of(place * height, 8), height), :]


def finish(chunk, count, blk, parts, local, arrived, pivot, factor, earlier, so_far):
    picked, width = local.shape
    order = pivot.shape[0]
    height = order // parts
    piece = jax.ShapeDtypeStruct((parts // 2, height, width), F32)
    operands = [blk[None], local, arrived, pivot, *factor, *earlier]
    in_specs = [SMEM] + [VMEM] * (len(operands) - 1)
    aliases = {}
    if so_far is not None:
        aliases = {len(operands): 0}
        operands.append(so_far)
        in_specs.append(ANY)
    return pl.pallas_call(
        functools.partial(finish_kernel, chunk, count),
        grid=(1,),
        in_specs=in_specs,
        out_specs=[pl.BlockSpec((picked, width), lambda i: (0, chunk)), VMEM, VMEM, VMEM],
        out_shape=[
            jax.ShapeDtypeStruct((picked, order), F32),
            jax.ShapeDtypeStruct((picked, width), F32),
            piece,
            piece,
        ],
        scratch_shapes=[pltpu.VMEM((order, width), F32)],
        input_output_aliases=aliases,
        compiler_params=params(20),
        cost_estimate=cost(5),
        name="finish",
    )(*operands)


def shards(ancestor_inv, lower_block, diag_inverse, row_index):
    grps, blks = lax.axis_size("grp"), lax.axis_size("blk")
    half = blks // 2
    tile, lower, names = ancestor_inv[0], lower_block[0], row_index[0]
    tile_rows, half_cols = tile.shape
    picked, order = lower.shape
    blk, grp = lax.axis_index("blk"), lax.axis_index("grp")
    side = grp % 2
    me = blk % half
    is_same = blk // half == side
    same = is_same.astype(jnp.int32)
    one = jnp.ones((), jnp.int32)
    chunks = 2
    width = order // chunks

    everyone = [(g, b) for g in range(grps) for b in range(blks)]
    sames = [(g, b) for g, b in everyone if b // half == g % 2]
    others = [(g, b) for g, b in everyone if b // half != g % 2]

    def move(x, pairs):
        perm = [(g * blks + b, h * blks + c) for (g, b), (h, c) in pairs]
        return lax.ppermute(x, ("grp", "blk"), perm)

    def across(x, who, stride):
        return move(x, [((g, b), (g, b ^ stride)) for g, b in who])

    def after(*arrays):
        return lax.optimization_barrier(arrays)

    onward = [((g, b), (g, b ^ half)) for g, b in sames] + [((g, b), (g ^ 1, b)) for g, b in others]
    backward = [(to, at) for at, to in onward]

    def on_core(x, who=everyone):
        return across(x, who, 1)

    def spread(arrays, who):
        arrays.update({p ^ 1: on_core(x, who) for p, x in list(arrays.items())})
        return [arrays[p] for p in range(half)]

    chips = [2 * s for s in range(half // 2)]

    def chip_gather(x, who):
        return {0: x} | {p: across(x, who, p) for p in chips[1:]}

    own = lax.optimization_barrier([lower[:, c * width : (c + 1) * width] for c in range(chunks)])
    high, low = chunks - 1, 0
    sent = {c: move(own[c], onward) for c in (high, low)}
    near = {high: chip_gather(own[high], sames)}
    sibling_names = lax.ppermute(names, "grp", [(g, g ^ 1) for g in range(grps)])
    pivot = lax.all_gather(diag_inverse[0], "blk", axis=0, tiled=True)

    group = max(1, 768 // tile_rows)
    while half % group:
        group //= 2

    def lists(which):
        rows = lax.dynamic_slice_in_dim(which, blk * picked, picked) - blk * tile_rows
        cols = lax.dynamic_slice_in_dim(which, side * half * picked, half * picked)
        cols = cols.reshape(half, picked) - (side * half + jnp.arange(half)[:, None]) * tile_rows
        return rows, cols + (jnp.arange(half)[:, None] % group) * tile_rows

    own_pick = pick(tile, *lists(names), group)
    sibling_names, own_pick, sent[high] = after(sibling_names, own_pick, sent[high])
    sib_pick, partial = second(
        same, me, tile, *lists(sibling_names), group, *own_pick, lower, chunks
    )

    def sum_cores(keep, send):
        got = on_core(send, others)
        return {i: keep[i] + got[i] for i in range(half // 2)}

    def sum_chips(places):
        for s in range(half.bit_length() - 2):
            for i in [i for i in places if i >> s & 1]:
                places[i ^ 1 << s] += across(places.pop(i), others, 2 << s)
        return places[0]

    sib_high = chip_gather(sent[high], sames)
    partial[high], sib_high, near[high], sent[low] = after(
        partial[high], sib_high, near[high], sent[low]
    )
    partial[low], sent[low] = after(partial[low], sent[low])
    sums = {c: sum_cores(*partial[c]) for c in (high, low)}
    away = {c: {i: x for i, x in sums[c].items() if i} for c in sums}
    away, sib_high = after(away, sib_high)
    back_sum = {c: sum_chips(away[c] | {0: sums[c][0]}) for c in (high, low)}
    sib = {high: spread(sib_high, sames)}
    sib_low = chip_gather(sent[low], sames)

    passed = {p: across(x, sames, half) for p, x in near[high].items() if p}
    high_parts = {p: jnp.where(is_same, x, passed[p]) if p else jnp.where(is_same, x, sent[high]) for p, x in near[high].items()}
    low_parts = chip_gather(jnp.where(is_same, own[low], sent[low]), everyone)

    result = apply(same, me, *sib_pick, sib[high])
    arrived = {high: move(jnp.where(is_same, result, back_sum[high]), backward)}
    result, sib_low = after(result, sib_low)
    sib[low], back_sum[low] = after(spread(sib_low, sames), back_sum[low])
    result = apply(same, me, *sib_pick, sib[low])
    arrived[low] = move(jnp.where(is_same, result, back_sum[low]), backward)

    result, high_parts, pivot = after(result, high_parts, pivot)

    height = order // blks
    gram_cols = lax.dynamic_slice_in_dim(pivot, blk * height, height, 1)
    gram = jnp.einsum("ar,ac->rc", gram_cols, pivot, precision=lax.Precision.HIGHEST)
    factor = factor_of(lower, pivot)
    local = apply(one, me, *own_pick, spread(high_parts, everyone))
    factor, gram, local = after(factor, gram, local)
    so_far, total, keep, send = finish(
        high, chunks, blk, blks, local, arrived[high], pivot, factor, [], None
    )

    def scatter(keep, send):
        left = keep + on_core(send)
        return left[0] + sum(across(left[q], everyone, 2 * q) for q in range(1, half))

    crosses = {high: scatter(keep, send)}
    total, low_parts, arrived[low] = after(total, low_parts, arrived[low])
    local = apply(one, me, *own_pick, spread(low_parts, everyone))
    so_far, _, keep, send = finish(
        low, chunks, blk, blks, local, arrived[low], pivot, factor, [total], so_far
    )
    crosses[low] = scatter(keep, send)

    cross = jnp.concatenate([crosses[c] for c in range(chunks)], axis=1)
    return so_far[None], (gram + cross)[None]


def solution(mesh):
    in_specs = (P("grp", "blk", None), P("grp", "blk", None), P("grp", "blk", None), P("grp", None))
    out_specs = (P("grp", "blk", None), P("grp", "blk", None))
    return jax.shard_map(shards, mesh=mesh, in_specs=in_specs, out_specs=out_specs, check_vma=False)
```

```python
import functools

import jax
import jax.numpy as jnp
from jax import lax
from jax.experimental import pallas as pl
from jax.experimental.pallas import tpu as pltpu
from jax.sharding import PartitionSpec as P

F32, BF16 = jnp.float32, jnp.bfloat16
TOP = 3.3895313892515355e38
COST = 3.3e6
DOWN, UP = 1.0 / 64.0, 64.0
NN = (((1,), (0,)), ((), ()))
VMEM = pl.BlockSpec(memory_space=pltpu.VMEM)
ANY = pl.BlockSpec(memory_space=pl.ANY)
HBM = pl.BlockSpec(memory_space=pltpu.HBM)
SMEM = pl.BlockSpec(memory_space=pltpu.SMEM)


def split(x):
    high = jnp.clip(x, -TOP, TOP).astype(BF16)
    return high, (x - high.astype(F32)).astype(BF16)


def dot1(a, b, dims=NN):
    return lax.dot_general(a, b, dims, preferred_element_type=F32)


def dot3(a, b, dims=NN):
    return dot1(a[0], b[0], dims) + dot1(a[0], b[1], dims) + dot1(a[1], b[0], dims)


def wide3(high, low, rhs):
    width = rhs[0].shape[1]
    pair = dot1(high, jnp.concatenate(rhs, axis=1))
    return pair[:, :width] + pair[:, width:] + dot1(low, rhs[0])


def cost(microseconds):
    return pl.CostEstimate(
        flops=0, bytes_accessed=int(microseconds * COST), transcendentals=0
    )


def params(mib):
    return pltpu.CompilerParams(vmem_limit_bytes=mib * 2**20)


def load_tile(tile_ref, slots, sems, step, steps):
    width = slots.shape[2]

    def copy(at):
        slot = at % 2
        source = tile_ref.at[:, pl.ds(pl.multiple_of(at * width, 128), width)]
        return pltpu.make_async_copy(source, slots.at[slot], sems.at[slot])

    @pl.when(step == 0)
    def _():
        copy(step).start()

    @pl.when(step + 1 < steps)
    def _():
        copy(step + 1).start()

    copy(step).wait()
    return slots[step % 2]


def hot_rows(rows_ref, hot_ref):
    at_row = lax.broadcasted_iota(jnp.int32, hot_ref.shape, 1)
    hot_ref[...] = (at_row == rows_ref[...]).astype(F32).astype(BF16)


def pick_rows(hot, piece):
    picked, height = hot.shape
    slack, deep = height - picked, 256
    if height != 3 * deep or slack > 2 * deep or picked % 16 or slack % 32:
        return dot1(hot, piece)
    until, since = deep, 2 * deep - slack
    first = dot1(hot[:until, :deep], piece[:deep])
    middle = dot1(hot[:, deep : 2 * deep], piece[deep : 2 * deep])
    last = dot1(hot[since:, 2 * deep :], piece[2 * deep :])
    return jnp.concatenate(
        [
            first[:since] + middle[:since],
            first[since:] + middle[since:until] + last[: until - since],
            middle[until:] + last[until - since :],
        ],
        axis=0,
    )


def pick_block(block, cols_ref, hot_ref, high_ref, low_ref):
    picked = hot_ref.shape[0]
    pair = split(block)
    both = jnp.concatenate([pick_rows(hot_ref[...], piece) for piece in pair], axis=0).astype(BF16)
    at_col = lax.broadcasted_iota(jnp.int32, (block.shape[1], picked), 0)
    for q in range(cols_ref.shape[0]):
        col_hot = (at_col == cols_ref[q]).astype(F32).astype(BF16)
        result = dot1(both, col_hot)
        high_ref[q] = result[:picked].astype(BF16)
        low_ref[q] = result[picked:].astype(BF16)


def pick_kernel(rows_ref, cols_ref, tile_ref, high_ref, low_ref, hot_ref, slots, sems):
    step = pl.program_id(0)

    @pl.when(step == 0)
    def _():
        hot_rows(rows_ref, hot_ref)

    block = load_tile(tile_ref, slots, sems, step, pl.num_programs(0))
    pick_block(block, cols_ref, hot_ref, high_ref, low_ref)


def pick(tile, rows, cols, group):
    height, all_cols = tile.shape
    blocks, picked = cols.shape
    width = all_cols // blocks * group
    out = jax.ShapeDtypeStruct((blocks, picked, picked), BF16)
    return pl.pallas_call(
        pick_kernel,
        grid=(blocks // group,),
        in_specs=[
            pl.BlockSpec((picked, 1), lambda i: (0, 0)),
            pl.BlockSpec((group, 1, picked), lambda i: (i, 0, 0)),
            HBM,
        ],
        out_specs=[pl.BlockSpec((group, picked, picked), lambda i: (i, 0, 0))] * 2,
        scratch_shapes=[
            pltpu.VMEM((picked, height), BF16),
            pltpu.VMEM((2, height, width), F32),
            pltpu.SemaphoreType.DMA((2,)),
        ],
        out_shape=[out] * 2,
        compiler_params=params(56),
        cost_estimate=cost(10),
        name="pick",
    )(rows[:, None], cols[:, None, :], tile)


def second_kernel(steps, info, rows_ref, cols_ref, tile_ref, q_high, q_low, lower_ref, *refs):
    high_ref, low_ref = refs[:2]
    hot_ref, slots, sems, lower_high, lower_low = refs[-5:]
    out_refs = refs[2:-5]
    chunks = len(out_refs) // 2
    width = lower_ref.shape[1] // chunks
    step = pl.program_id(0)

    @pl.when((info[0] == 1) & (step == 0))
    def _():
        hot_rows(rows_ref, hot_ref)

    @pl.when((info[0] == 1) & (step < steps))
    def _():
        block = load_tile(tile_ref, slots, sems, step, steps)
        pick_block(block, cols_ref, hot_ref, high_ref, low_ref)

    @pl.when((info[0] == 0) & (step == 0))
    def _():
        lower_high[...], lower_low[...] = split(lower_ref[...] * DOWN)

    @pl.when(info[0] == 0)
    def _():
        high, low = jnp.transpose(q_high[0]), jnp.transpose(q_low[0])
        full = dot1(high, lower_high[...]) + dot1(high, lower_low[...]) + dot1(low, lower_high[...])
        for parity in range(2):

            @pl.when(step % 2 == parity)
            def _(parity=parity):
                for c in range(chunks):
                    out_refs[2 * c + parity][0] = full[:, c * width : (c + 1) * width]


def second(same, me, tile, rows, cols, group, high, low, lower, chunks):
    height, all_cols = tile.shape
    blocks, picked = cols.shape
    total = lower.shape[1]
    width = all_cols // blocks * group
    steps = blocks // group
    out = jax.ShapeDtypeStruct((blocks, picked, picked), BF16)
    back = jax.ShapeDtypeStruct((blocks // 2, picked, total // chunks), F32)

    def at_pick(p, info):
        return (jnp.minimum(p, steps - 1) * info[0], 0, 0)

    def at_block(p, info):
        return (lax.bitwise_xor(info[1], p * (1 - info[0])), 0, 0)

    def at_back(p, info):
        return (p // 2 * (1 - info[0]), 0, 0)

    flat = pl.pallas_call(
        functools.partial(second_kernel, steps),
        grid_spec=pltpu.PrefetchScalarGridSpec(
            num_scalar_prefetch=1,
            grid=(blocks,),
            in_specs=[
                pl.BlockSpec((picked, 1), lambda p, info: (0, 0)),
                pl.BlockSpec((group, 1, picked), at_pick),
                HBM,
                pl.BlockSpec((1, picked, picked), at_block),
                pl.BlockSpec((1, picked, picked), at_block),
                pl.BlockSpec((picked, total), lambda p, info: (0, 0)),
            ],
            out_specs=[pl.BlockSpec((group, picked, picked), at_pick)] * 2
            + [pl.BlockSpec((1, picked, total // chunks), at_back)] * (2 * chunks),
            scratch_shapes=[
                pltpu.VMEM((picked, height), BF16),
                pltpu.VMEM((2, height, width), F32),
                pltpu.SemaphoreType.DMA((2,)),
            ]
            + [pltpu.VMEM((picked, total), BF16)] * 2,
        ),
        out_shape=[out] * 2 + [back] * (2 * chunks),
        compiler_params=params(56),
        cost_estimate=cost(10),
        name="second",
    )(jnp.stack([same, me]), rows[:, None], cols[:, None, :], tile, high, low, lower)
    return flat[:2], [(flat[2 + 2 * c], flat[3 + 2 * c]) for c in range(chunks)]


def apply_kernel(info, high_ref, low_ref, *refs):
    pieces, out_ref = refs[:-1], refs[-1]
    step = pl.program_id(0)

    @pl.when(info[0] == 1)
    def _():
        for p, piece in enumerate(pieces):

            @pl.when(step == p)
            def _(p=p, piece=piece):
                part = wide3(high_ref[0], low_ref[0], split(piece[...] * DOWN))
                out_ref[...] = part if p == 0 else out_ref[...] + part


def apply(active, me, high, low, pieces):
    blocks, picked, _ = high.shape
    width = pieces[0].shape[1]
    block = pl.BlockSpec(
        (1, picked, picked), lambda p, info: (lax.bitwise_xor(info[1], p * info[0]), 0, 0)
    )
    whole = pl.BlockSpec((picked, width), lambda p, info: (0, 0))
    return pl.pallas_call(
        apply_kernel,
        grid_spec=pltpu.PrefetchScalarGridSpec(
            num_scalar_prefetch=1,
            grid=(blocks,),
            in_specs=[block, block] + [whole] * blocks,
            out_specs=whole,
        ),
        out_shape=jax.ShapeDtypeStruct((picked, width), F32),
        compiler_params=params(12),
        cost_estimate=cost(4.5),
        name="apply",
    )(jnp.stack([active, me]), high, low, *pieces)


def factor_kernel(lower_ref, pivot_ref, high_ref, low_ref):
    full = dot3(split(lower_ref[...]), split(pivot_ref[...]))
    high_ref[...], low_ref[...] = split(jnp.transpose(full))


def factor_of(lower, pivot):
    out = jax.ShapeDtypeStruct(lower.shape[::-1], BF16)
    return pl.pallas_call(
        factor_kernel,
        in_specs=[VMEM, VMEM],
        out_specs=[VMEM, VMEM],
        out_shape=[out, out],
        compiler_params=params(16),
        cost_estimate=cost(2.2),
        name="factor",
    )(lower, pivot)


def finish_kernel(chunk, count, info, *refs):
    local_ref, arrived_ref, pivot_ref, high_ref, low_ref = refs[:5]
    earlier = refs[5 : 5 + count - 1 - chunk]
    rows_ref, sum_ref, keep_ref, send_ref, cross_ref = refs[-5:]
    width = local_ref.shape[1]
    at = chunk * width
    mine = local_ref[...] + arrived_ref[...]
    sum_ref[...] = mine
    result = dot3(split(mine), split(pivot_ref[at : at + width, at : at + width]))
    for k, ref in enumerate(earlier):
        low_at = (chunk + 1 + k) * width
        result += dot3(split(ref[...]), split(pivot_ref[low_at : low_at + width, at : at + width]))
    result = result * UP
    rows_ref[...] = -result
    cross_ref[...] = dot3((high_ref[...], low_ref[...]), split(result))
    height = keep_ref.shape[1]
    for q in range(keep_ref.shape[0]):
        for parity, ref in enumerate((keep_ref, send_ref)):
            place = lax.bitwise_xor(info[0], 2 * q + parity)
            ref[q] = cross_ref[pl.ds(pl.multiple_of(place * height, 8), height), :]


def finish(chunk, count, blk, parts, local, arrived, pivot, factor, earlier, so_far):
    picked, width = local.shape
    order = pivot.shape[0]
    height = order // parts
    piece = jax.ShapeDtypeStruct((parts // 2, height, width), F32)
    operands = [blk[None], local, arrived, pivot, *factor, *earlier]
    in_specs = [SMEM] + [VMEM] * (len(operands) - 1)
    aliases = {}
    if so_far is not None:
        aliases = {len(operands): 0}
        operands.append(so_far)
        in_specs.append(ANY)
    return pl.pallas_call(
        functools.partial(finish_kernel, chunk, count),
        grid=(1,),
        in_specs=in_specs,
        out_specs=[pl.BlockSpec((picked, width), lambda i: (0, chunk)), VMEM, VMEM, VMEM],
        out_shape=[
            jax.ShapeDtypeStruct((picked, order), F32),
            jax.ShapeDtypeStruct((picked, width), F32),
            piece,
            piece,
        ],
        scratch_shapes=[pltpu.VMEM((order, width), F32)],
        input_output_aliases=aliases,
        compiler_params=params(20),
        cost_estimate=cost(5),
        name="finish",
    )(*operands)


def shards(ancestor_inv, lower_block, diag_inverse, row_index):
    grps, blks = lax.axis_size("grp"), lax.axis_size("blk")
    half = blks // 2
    tile, lower, names = ancestor_inv[0], lower_block[0], row_index[0]
    tile_rows, half_cols = tile.shape
    picked, order = lower.shape
    blk, grp = lax.axis_index("blk"), lax.axis_index("grp")
    side = grp % 2
    me = blk % half
    is_same = blk // half == side
    same = is_same.astype(jnp.int32)
    one = jnp.ones((), jnp.int32)
    chunks = 2
    width = order // chunks

    everyone = [(g, b) for g in range(grps) for b in range(blks)]
    sames = [(g, b) for g, b in everyone if b // half == g % 2]
    others = [(g, b) for g, b in everyone if b // half != g % 2]

    def move(x, pairs):
        perm = [(g * blks + b, h * blks + c) for (g, b), (h, c) in pairs]
        return lax.ppermute(x, ("grp", "blk"), perm)

    def across(x, who, stride):
        return move(x, [((g, b), (g, b ^ stride)) for g, b in who])

    def after(*arrays):
        return lax.optimization_barrier(arrays)

    onward = [((g, b), (g, b ^ half)) for g, b in sames] + [((g, b), (g ^ 1, b)) for g, b in others]
    backward = [(to, at) for at, to in onward]

    def on_core(x, who=everyone):
        return across(x, who, 1)

    def spread(arrays, who):
        arrays.update({p ^ 1: on_core(x, who) for p, x in list(arrays.items())})
        return [arrays[p] for p in range(half)]

    chips = [2 * s for s in range(half // 2)]

    def chip_gather(x, who):
        return {0: x} | {p: across(x, who, p) for p in chips[1:]}

    own = lax.optimization_barrier([lower[:, c * width : (c + 1) * width] for c in range(chunks)])
    high, low = chunks - 1, 0
    sent = {c: move(own[c], onward) for c in (high, low)}
    near = {high: chip_gather(own[high], sames)}
    sibling_names = lax.ppermute(names, "grp", [(g, g ^ 1) for g in range(grps)])
    pivot = lax.all_gather(diag_inverse[0], "blk", axis=0, tiled=True)

    group = max(1, 768 // tile_rows)
    while half % group:
        group //= 2

    def lists(which):
        rows = lax.dynamic_slice_in_dim(which, blk * picked, picked) - blk * tile_rows
        cols = lax.dynamic_slice_in_dim(which, side * half * picked, half * picked)
        cols = cols.reshape(half, picked) - (side * half + jnp.arange(half)[:, None]) * tile_rows
        return rows, cols + (jnp.arange(half)[:, None] % group) * tile_rows

    own_pick = pick(tile, *lists(names), group)
    sibling_names, own_pick, sent[high] = after(sibling_names, own_pick, sent[high])
    sib_pick, partial = second(
        same, me, tile, *lists(sibling_names), group, *own_pick, lower, chunks
    )

    def sum_cores(keep, send):
        got = on_core(send, others)
        return {i: keep[i] + got[i] for i in range(half // 2)}

    def sum_chips(places):
        for s in range(half.bit_length() - 2):
            for i in [i for i in places if i >> s & 1]:
                places[i ^ 1 << s] += across(places.pop(i), others, 2 << s)
        return places[0]

    sib_high = chip_gather(sent[high], sames)
    partial[high], sib_high, near[high], sent[low] = after(
        partial[high], sib_high, near[high], sent[low]
    )
    partial[low], sent[low] = after(partial[low], sent[low])
    sums = {c: sum_cores(*partial[c]) for c in (high, low)}
    away = {c: {i: x for i, x in sums[c].items() if i} for c in sums}
    away, sib_high = after(away, sib_high)
    back_sum = {c: sum_chips(away[c] | {0: sums[c][0]}) for c in (high, low)}
    sib = {high: spread(sib_high, sames)}
    sib_low = chip_gather(sent[low], sames)

    passed = {p: across(x, sames, half) for p, x in near[high].items() if p}
    high_parts = {p: jnp.where(is_same, x, passed[p]) if p else jnp.where(is_same, x, sent[high]) for p, x in near[high].items()}
    low_parts = chip_gather(jnp.where(is_same, own[low], sent[low]), everyone)

    result = apply(same, me, *sib_pick, sib[high])
    arrived = {high: move(jnp.where(is_same, result, back_sum[high]), backward)}
    result, sib_low = after(result, sib_low)
    sib[low], back_sum[low] = after(spread(sib_low, sames), back_sum[low])
    result = apply(same, me, *sib_pick, sib[low])
    arrived[low] = move(jnp.where(is_same, result, back_sum[low]), backward)

    result, high_parts, pivot = after(result, high_parts, pivot)

    height = order // blks
    gram_cols = lax.dynamic_slice_in_dim(pivot, blk * height, height, 1)
    gram = jnp.einsum("ar,ac->rc", gram_cols, pivot, precision=lax.Precision.HIGH)
    factor = factor_of(lower, pivot)
    local = apply(one, me, *own_pick, spread(high_parts, everyone))
    factor, gram, local = after(factor, gram, local)
    so_far, total, keep, send = finish(
        high, chunks, blk, blks, local, arrived[high], pivot, factor, [], None
    )

    def scatter(keep, send):
        left = keep + on_core(send)
        return left[0] + sum(across(left[q], everyone, 2 * q) for q in range(1, half))

    crosses = {high: scatter(keep, send)}
    total, low_parts, arrived[low] = after(total, low_parts, arrived[low])
    local = apply(one, me, *own_pick, spread(low_parts, everyone))
    so_far, _, keep, send = finish(
        low, chunks, blk, blks, local, arrived[low], pivot, factor, [total], so_far
    )
    crosses[low] = scatter(keep, send)

    cross = jnp.concatenate([crosses[c] for c in range(chunks)], axis=1)
    return so_far[None], (gram + cross)[None]


def solution(mesh):
    in_specs = (P("grp", "blk", None), P("grp", "blk", None), P("grp", "blk", None), P("grp", None))
    out_specs = (P("grp", "blk", None), P("grp", "blk", None))
    return jax.shard_map(shards, mesh=mesh, in_specs=in_specs, out_specs=out_specs, check_vma=False)
```
